256 devices in a mesh: blk: 64 (over x_lo, z, y), grp: 4 (over x_hi, core).
Axes of the slice: x: 4 (x_hi: 2, x_lo: 2; x = x_hi * 2 + x_lo), y: 4, z: 8, core: 2. Of those that a mesh axis runs over, the one named last changes fastest.
Arguments:
- embedding: bfloat16 [131072, 256], P('blk'), may hold values from -1.5 to 1.5
- adjacency: int32 [4, 16384, 2048], P(None, 'blk', 'grp'), may hold values from 0 to 255
- owners: int32 [64], replicated, may hold values from 0 to 63, each once
Outputs:
- gradient: float32 [131072, 256], P(('blk', 'grp'))
The draws below stay inside these ranges and needn't reach their ends.
Inputs may be any that keep to these rules, and one draw needn't show every extreme that they name: `owners`: entries 0 to 3 are distinct block indices; later entries are not read.
All inputs are finite; a program needn't handle non-finite values.
Results may differ from the reference program's by a relative error of at most 0.00044.
Values may be sent and summed in bfloat16 or wider, within the bound.
No kernel may reach another device: no remote copies, remote signals or barrier semaphores. Data moves between devices by JAX's collectives and lax.ppermute only.
A program may use at most 128 MiB of HBM per device.

```python
import jax
import jax.numpy as jnp
from jax import lax

W = 256
R = 2048
SECTIONS = 4
NODES = 131072
N_BLK = 64


def place_ends(drawn, own_key, low, largest):
    index_at = [jax.random.randint(jax.random.fold_in(own_key, axis), (), 0, length) for axis, length in enumerate(drawn.shape)]
    main_axis = drawn.shape.index(max(drawn.shape))
    neighbour = index_at[:main_axis] + [(index_at[main_axis] + 1) % drawn.shape[main_axis]] + index_at[main_axis + 1:]
    return drawn.at[tuple(index_at)].set(low).at[tuple(neighbour)].set(largest)


def level_of(key, shape, shards, smallest, high):
    loudness, own = 1.0, jax.random.fold_in(key, 6)
    for dim, shards_of in shards:
        steps = jnp.exp(jax.random.uniform(jax.random.fold_in(own, dim), (shards_of,), jnp.float32, smallest / len(shards), high / len(shards)))
        loudness = loudness * jnp.repeat(steps, shape[dim] // shards_of).reshape([-1 if axis == dim else 1 for axis in range(len(shape))])
    return loudness


def bell_draw(own_key, extent, deviation, limit, cuts=(), held_as=jnp.bfloat16):
    array = deviation * jax.random.normal(own_key, extent, jnp.float32)
    if cuts:
        array = array * level_of(own_key, extent, cuts, -0.22, 0.18)
    return jnp.clip(array, -limit, limit).astype(held_as)


def setup_inputs(seed: int = 0) -> dict:
    streams_of = jax.random.split(jax.random.key(seed), 4)
    embedding = bell_draw(streams_of[0], (NODES, W), 0.25, 1.5, ((0, 64),))
    adjacency = place_ends(jax.random.randint(streams_of[1], (SECTIONS, NODES // 8, R), 0, 256), jax.random.fold_in(streams_of[1], 1), 0, 255).astype(jnp.int32)
    owners = jax.random.permutation(streams_of[2], N_BLK).astype(jnp.int32)
    return {"embedding": embedding, "adjacency": adjacency, "owners": owners}


def reference(embedding, adjacency, owners):
    shifts = jnp.arange(8, dtype=jnp.int32)
    blocks = embedding.reshape(N_BLK, R, W)
    words = adjacency.reshape(SECTIONS, N_BLK, R // 8, R)
    row_total = jnp.zeros((N_BLK, R, W), jnp.float32)
    col_total = jnp.zeros((N_BLK, R, W), jnp.float32)
    for section in range(SECTIONS):
        start = (owners[section] * R).astype(jnp.int32)
        block = lax.dynamic_slice_in_dim(embedding, start, R, 0)

        def one(carry, item):
            rows_here, word_here = item
            bits = (jnp.right_shift(word_here[:, None, :], shifts[None, :, None]) & 1).reshape(R, R).astype(jnp.float32)
            scores = jnp.dot(rows_here, block.T, preferred_element_type=jnp.float32)
            error = (jax.nn.sigmoid(scores) - bits).astype(jnp.bfloat16)
            rowg = jnp.dot(error, block, preferred_element_type=jnp.float32)
            colg = carry + jnp.dot(error.T, rows_here, preferred_element_type=jnp.float32)
            return colg, rowg

        colg, rowg = lax.scan(one, jnp.zeros((R, W), jnp.float32), (blocks, words[section]))
        row_total = row_total + rowg
        picked = (jnp.arange(N_BLK, dtype=jnp.int32) == owners[section]).astype(jnp.float32)
        col_total = col_total + picked[:, None, None] * colg[None]
    return ((row_total + col_total) * (R ** -0.5)).reshape(NODES, W)
```

```python
import functools

import jax
import jax.numpy as jnp
from jax import lax
from jax.experimental import pallas as pl
from jax.experimental.pallas import tpu as pltpu
from jax.sharding import PartitionSpec as P

TILE = 256
PLANES = 8
WORDS = TILE // PLANES
VMEM_LIMIT = 48 * 1024 * 1024


def arrange_kernel(emb_ref, rows_ref, cols_ref):
    new = lax.broadcasted_iota(jnp.int32, (TILE, TILE), 0)
    old = lax.broadcasted_iota(jnp.int32, (TILE, TILE), 1)
    pick = old == (new & (WORDS - 1)) * PLANES + new // WORDS
    order = jnp.where(pick, 1.0, 0.0).astype(jnp.bfloat16)
    for tile in range(emb_ref.shape[0] // TILE):
        span = slice(tile * TILE, (tile + 1) * TILE)
        moved = jnp.dot(order, emb_ref[span, :], preferred_element_type=jnp.float32)
        rows_ref[span, :] = moved.astype(jnp.bfloat16)
        cols_ref[:, span] = moved.T.astype(jnp.bfloat16)


def half_kernel(first, *refs):
    if first:
        half_ref, rows_ref, cols_ref, block_ref, words_ref, row_ref, col_ref = refs
        prior_ref = None
    else:
        half_ref, rows_ref, cols_ref, block_ref, words_ref, prior_ref, row_ref, col_ref = refs
    sections = words_ref.shape[0]
    wide = block_ref.shape[0]
    each = wide // sections
    start = pl.multiple_of(half_ref[0] * each, each)
    block = block_ref[...]
    halved = block * jnp.bfloat16(0.5)
    for tile in range(rows_ref.shape[0] // TILE):
        span = slice(tile * TILE, (tile + 1) * TILE)
        here = rows_ref[span, :]
        scores = lax.dot_general(
            here, halved, (((1,), (1,)), ((), ())), preferred_element_type=jnp.float32
        )
        parts = []
        for section in range(sections):
            words = words_ref[section, pl.ds(tile * WORDS, WORDS), pl.ds(start, each)]
            planes = []
            for plane in range(PLANES):
                part = scores[plane * WORDS : (plane + 1) * WORDS, section * each : (section + 1) * each]
                sign = jnp.where((words & (1 << plane)) == 0, 1.0, -1.0)
                planes.append((jnp.tanh(part) + sign).astype(jnp.bfloat16))
            parts.append(jnp.concatenate(planes, axis=0))
        error = jnp.concatenate(parts, axis=1)
        row = jnp.dot(error, block, preferred_element_type=jnp.float32)
        if prior_ref is not None:
            row = row + prior_ref[span, :]
        row_ref[span, :] = row
        col = jnp.dot(cols_ref[:, span], error, preferred_element_type=jnp.float32)
        if tile == 0:
            col_ref[...] = col
        else:
            col_ref[...] += col


def vmem(count):
    return [pl.BlockSpec(memory_space=pltpu.VMEM)] * count


def arrange(embedding):
    rows, width = embedding.shape
    return pl.pallas_call(
        arrange_kernel,
        out_shape=(
            jax.ShapeDtypeStruct((rows, width), jnp.bfloat16),
            jax.ShapeDtypeStruct((width, rows), jnp.bfloat16),
        ),
        in_specs=vmem(1),
        out_specs=tuple(vmem(2)),
        compiler_params=pltpu.CompilerParams(vmem_limit_bytes=VMEM_LIMIT),
    )(embedding)


def half_products(half, by_row, by_col, block, words, prior):
    rows, width = by_row.shape
    wide = block.shape[0]
    first = prior is None
    args = (half, by_row, by_col, block, words) + (() if first else (prior,))
    flops = 3 * 2 * rows * wide * width
    return pl.pallas_call(
        functools.partial(half_kernel, first),
        out_shape=(
            jax.ShapeDtypeStruct((rows, width), jnp.float32),
            jax.ShapeDtypeStruct((width, wide), jnp.float32),
        ),
        in_specs=[pl.BlockSpec(memory_space=pltpu.SMEM)] + vmem(len(args) - 1),
        out_specs=tuple(vmem(2)),
        cost_estimate=pl.CostEstimate(flops=flops, bytes_accessed=8 << 20, transcendentals=rows * wide),
        compiler_params=pltpu.CompilerParams(vmem_limit_bytes=VMEM_LIMIT),
    )(*args)


def body(embedding, adjacency, owners):
    rows, width = embedding.shape
    sections = adjacency.shape[0]
    groups = lax.axis_size("grp")
    blocks = lax.axis_size("blk")
    quarter = rows // groups
    near = blocks // 2
    mine = lax.axis_index("blk")
    place = lax.axis_index("grp")
    side = mine // near
    core = place % 2
    high = place // 2
    flip_side = [(b, (b + near) % blocks) for b in range(blocks)]
    planes_zy = [list(range(x * near, (x + 1) * near)) for x in range(2)]

    own = lax.dynamic_slice_in_dim(embedding, place * quarter, quarter, 0)
    piece = quarter // blocks
    got = lax.all_to_all(own.reshape(blocks, piece, width), "blk", 0, 0)
    picked = jnp.stack([lax.dynamic_index_in_dim(got, owners[s], 0, keepdims=False) for s in range(sections)])
    spread = jnp.broadcast_to(picked[None], (near,) + picked.shape)
    half = lax.all_to_all(spread, "blk", 0, 0, axis_index_groups=planes_zy)
    near_block = half.transpose(1, 0, 2, 3).reshape(sections * quarter // 2, width)
    far_block = lax.ppermute(near_block, "blk", flip_side)

    by_row, by_col = arrange(embedding)
    row, near_col = half_products(side.reshape(1), by_row, by_col, near_block, adjacency, None)
    sent_col = lax.ppermute(near_col, "blk", flip_side)
    row, far_col = half_products(1 - side.reshape(1), by_row, by_col, far_block, adjacency, row)

    row = row.reshape(2, 2, quarter, width)
    away = lax.dynamic_index_in_dim(row, 1 - core, 1, keepdims=False)
    kept = lax.dynamic_index_in_dim(row, core, 1, keepdims=False)
    kept = kept + lax.ppermute(away, "grp", [(g, g ^ 1) for g in range(groups)])
    away = lax.dynamic_index_in_dim(kept, 1 - high, 0, keepdims=False)
    mine_row = lax.dynamic_index_in_dim(kept, high, 0, keepdims=False)
    mine_row = mine_row + lax.ppermute(away, "grp", [(g, g ^ 2) for g in range(groups)])

    col = (far_col + sent_col).reshape(near, width // near, sections * quarter // 2)
    col = lax.all_to_all(col, "blk", 0, 0, axis_index_groups=planes_zy)
    col = col.sum(axis=0).reshape(width // near, sections, quarter // 2)
    target = jnp.arange(blocks, dtype=jnp.int32)
    out = jnp.zeros((blocks, width // near, quarter // 2), jnp.float32)
    for s in range(sections):
        out = jnp.where((target == owners[s])[:, None, None], col[:, s][None], out)
    back = lax.all_to_all(out, "blk", 0, 0)
    back = back.reshape(2, width, quarter // 2)[::-1]
    owned = jnp.any(owners[:sections] == mine)
    side_col = back.transpose(0, 2, 1).reshape(quarter, width)
    mine_row = mine_row.reshape(quarter // TILE, PLANES, WORDS, width).transpose(0, 2, 1, 3).reshape(quarter, width)
    return (mine_row + jnp.where(owned, side_col, 0.0)) * (0.5 * rows ** (-0.5))


def solution(mesh):
    return jax.shard_map(
        body,
        mesh=mesh,
        in_specs=(P("blk", None), P(None, "blk", "grp"), P()),
        out_specs=P(("blk", "grp"), None),
        check_vma=False,
    )
```

```python
import functools

import jax
import jax.numpy as jnp
from jax import lax
from jax.experimental import pallas as pl
from jax.experimental.pallas import tpu as pltpu
from jax.sharding import PartitionSpec as P

TILE = 256
PLANES = 8
WORDS = TILE // PLANES
SECTIONS = 4
LINE = 8

ANYWHERE = pl.BlockSpec(memory_space=pltpu.HBM)
SCALARS = pl.BlockSpec(memory_space=pltpu.SMEM)
VECTORS = pl.BlockSpec(memory_space=pltpu.VMEM)


def local_call(kernel, outs, ins, scratch=(), cost=None, limit=32):
    return pl.pallas_call(
        kernel,
        out_shape=outs,
        in_specs=ins,
        out_specs=jax.tree.map(lambda _: VECTORS, outs),
        scratch_shapes=scratch,
        cost_estimate=cost,
        compiler_params=pltpu.CompilerParams(vmem_limit_bytes=limit << 20),
    )


def own_kernel(owners_ref, emb_ref, own_ref, list_ref, held_ref, sem):
    blocks, deep, lanes = own_ref.shape
    quarter, width = held_ref.shape
    start = lax.axis_index("grp") * quarter
    rows = pl.ds(pl.multiple_of(start, quarter), quarter)
    copy = pltpu.make_async_copy(emb_ref.at[rows, :], held_ref, sem.at[0])
    names = pltpu.make_async_copy(owners_ref, list_ref, sem.at[1])
    copy.start()
    names.start()
    copy.wait()
    chunks = quarter // deep
    for part in range(width // lanes):
        for chunk in range(chunks):
            own_ref[part * chunks + chunk] = held_ref[
                chunk * deep : (chunk + 1) * deep, part * lanes : (part + 1) * lanes
            ]
    names.wait()


def to_line_kernel(owners_ref, got_ref, sent_ref):
    for s in range(SECTIONS):
        held = got_ref[owners_ref[s]]
        for part in range(sent_ref.shape[0]):
            sent_ref[part, s] = held


def to_plane_kernel(came_ref, sent_ref):
    held = came_ref[...]
    for part in range(sent_ref.shape[0]):
        sent_ref[part] = held


def products_kernel(
    emb_ref, pieces_ref, far_words_ref, keep_ref, send_ref, col_ref,
    block_ref, halved_ref, rows_ref, cols_ref, error_ref, words_ref, sem,
):
    plane, line, sections, deep, lanes = pieces_ref.shape
    rows, width = emb_ref.shape
    fetch = pltpu.make_async_copy(far_words_ref, words_ref, sem)
    fetch.start()
    quarter = rows // 4
    place = lax.axis_index("grp")
    core, high = place % 2, place // 2
    for section in range(sections):
        for z in range(line):
            for xy in range(plane):
                at = section * quarter + (z * 4 + xy % 4) * deep
                span = slice(at, at + deep)
                cut = slice(xy // 4 * lanes, (xy // 4 + 1) * lanes)
                value = pieces_ref[xy, z, section]
                block_ref[span, cut] = value
                halved_ref[span, cut] = value * jnp.bfloat16(0.5)

    new = lax.broadcasted_iota(jnp.int32, (TILE, TILE), 0)
    old = lax.broadcasted_iota(jnp.int32, (TILE, TILE), 1)
    pick = old == (new % WORDS) * PLANES + new // WORDS
    order = jnp.where(pick, 1.0, 0.0).astype(jnp.bfloat16)
    source = (new // 128) * 128 + (new // 4 % 8) * 16 + (new // 32 % 4) * 4 + new % 4
    spread = jnp.where(old == source, 1.0, 0.0).astype(jnp.bfloat16)

    tiles = []
    for away in (1, 0):
        for other in (0, 1):
            for sub in range(2):
                tiles.append(((high ^ other) * 2 + (core ^ away)) * 2 + sub)
    for step, tile in enumerate(tiles):
        span = slice(step * TILE, (step + 1) * TILE)
        raw = emb_ref[pl.ds(pl.multiple_of(tile * TILE, TILE), TILE), :]
        here = jnp.dot(order, raw, preferred_element_type=jnp.float32).astype(jnp.bfloat16)
        rows_ref[span, :] = here
        cols_ref[:, span] = lax.dot_general(
            spread, here, (((1,), (1,)), ((), ())), preferred_element_type=jnp.float32
        ).astype(jnp.bfloat16)
    fetch.wait()
    for pair in range(4):
        span = slice(pair * 2 * TILE, (pair + 1) * 2 * TILE)
        for section in range(sections):
            cut = slice(section * quarter, (section + 1) * quarter)
            scores = lax.dot_general(
                rows_ref[span, :], halved_ref[cut, :], (((1,), (1,)), ((), ())), preferred_element_type=jnp.float32
            )
            for sub in range(2):
                tile = tiles[pair * 2 + sub]
                words = words_ref[section, pl.ds(pl.multiple_of(tile * WORDS, WORDS), WORDS), :]
                for plane in range(PLANES):
                    at = sub * TILE + plane * WORDS
                    sign = jnp.where((words & (1 << plane)) == 0, 1.0, -1.0)
                    error = jnp.tanh(scores[at : at + WORDS, :]) + sign
                    error_ref[pair * 2 * TILE + at : pair * 2 * TILE + at + WORDS, cut] = error.astype(jnp.bfloat16)
        row = jnp.dot(error_ref[span, :], block_ref[...], preferred_element_type=jnp.float32)
        store = keep_ref if pair // 2 else send_ref
        store[pair % 2] = row
    for section in range(sections):
        cut = slice(section * quarter, (section + 1) * quarter)
        col_ref[:, cut] = jnp.dot(cols_ref[...], error_ref[:, cut], preferred_element_type=jnp.float32)


def to_line_sum_kernel(came_ref, out_ref):
    total = came_ref[0]
    for part in range(1, came_ref.shape[0]):
        total = total + came_ref[part]
    deep = out_ref.shape[1]
    for part in range(out_ref.shape[0]):
        out_ref[part] = total[part * deep : (part + 1) * deep, :]


def to_owner_kernel(owners_ref, came_ref, out_ref):
    total = came_ref[0]
    for part in range(1, came_ref.shape[0]):
        total = total + came_ref[part]
    out_ref[...] = jnp.zeros_like(out_ref)
    quarter = out_ref.shape[2]
    for s in range(SECTIONS):
        out_ref[owners_ref[s]] = total[:, s * quarter : (s + 1) * quarter]


def finish_kernel(scale, owners_ref, keep_ref, came_ref, back_ref, out_ref, row_ref):
    mine = lax.axis_index("blk")
    owned = jnp.bool_(False)
    for s in range(SECTIONS):
        owned = owned | (owners_ref[s] == mine)
    quarter, width = out_ref.shape
    blocks, deep, _ = back_ref.shape
    row = keep_ref[0] + came_ref[...].astype(jnp.float32)
    for tile in range(quarter // TILE):
        for plane in range(PLANES):
            at = tile * TILE + plane * WORDS
            for lane in range(width // 128):
                row_ref[lane, pl.ds(tile * TILE + plane, WORDS, stride=PLANES), :] = row[
                    at : at + WORDS, lane * 128 : (lane + 1) * 128
                ]
    for lane in range(width // 128):
        out_ref[:, lane * 128 : (lane + 1) * 128] = row_ref[lane] * scale

    @pl.when(owned)
    def _():
        col = back_ref[...].reshape(blocks * deep, quarter)
        out_ref[...] += col.T * scale


def body(embedding, adjacency, owners):
    rows, width = embedding.shape
    sections = adjacency.shape[0]
    groups = lax.axis_size("grp")
    blocks = lax.axis_size("blk")
    quarter = rows // groups
    wide = sections * quarter
    plane_xy = [[x * 32 + z * 4 + y for x in range(2) for y in range(4)] for z in range(LINE)]
    line_z = [[x * 32 + z * 4 + y for z in range(LINE)] for x in range(2) for y in range(4)]

    def swap(value, line=None):
        return lax.all_to_all(value, "blk", 0, 0, axis_index_groups=line)

    def shape(*extent, dtype=jnp.float32):
        return jax.ShapeDtypeStruct(extent, dtype)

    half = jnp.bfloat16
    deep, lanes = 2 * quarter // blocks, width // 2
    own, owners = local_call(
        own_kernel,
        (shape(blocks, deep, lanes, dtype=half), shape(blocks, dtype=jnp.int32)),
        [ANYWHERE, ANYWHERE],
        [pltpu.VMEM((quarter, width), half), pltpu.SemaphoreType.DMA((2,))],
        limit=60,
    )(owners, embedding)
    got = swap(own)
    sent = local_call(to_line_kernel, shape(LINE, sections, deep, lanes, dtype=half), [SCALARS, VECTORS])(owners, got)
    came = swap(sent, line_z)
    spread = local_call(to_plane_kernel, shape(LINE, LINE, sections, deep, lanes, dtype=half), [VECTORS])(came)
    pieces = swap(spread, plane_xy)

    keep, send, col = local_call(
        products_kernel,
        (shape(2, quarter, width), shape(2, quarter, width), shape(width, wide)),
        [VECTORS, VECTORS, ANYWHERE],
        [
            pltpu.VMEM((wide, width), half),
            pltpu.VMEM((wide, width), half),
            pltpu.VMEM((rows, width), half),
            pltpu.VMEM((width, rows), half),
            pltpu.VMEM((rows, wide), half),
            pltpu.VMEM(adjacency.shape, jnp.int32),
            pltpu.SemaphoreType.DMA,
        ],
        pl.CostEstimate(flops=6 * rows * wide * width, bytes_accessed=9 << 20, transcendentals=rows * wide),
        limit=32,
    )(embedding, pieces, adjacency)

    keep = keep + lax.ppermute(send, "grp", [(g, g ^ 1) for g in range(groups)])
    came = lax.ppermute(keep[1].astype(jnp.float16), "grp", [(g, g ^ 2) for g in range(groups)]).astype(jnp.float32)
    col = swap(col.astype(jnp.float16).reshape(LINE, width // LINE, wide), plane_xy).astype(jnp.float32)
    col = local_call(to_line_sum_kernel, shape(LINE, width // blocks, wide), [VECTORS])(col)
    col = swap(col, line_z)
    col = local_call(to_owner_kernel, shape(blocks, width // blocks, quarter), [SCALARS, VECTORS])(owners, col)
    back = swap(col)
    return local_call(
        functools.partial(finish_kernel, 0.5 * rows ** (-0.5)),
        shape(quarter, width),
        [SCALARS, VECTORS, VECTORS, VECTORS],
        [pltpu.VMEM((width // 128, quarter, 128), jnp.float32)],
    )(owners, keep, came, back)


def solution(mesh):
    return jax.shard_map(
        body,
        mesh=mesh,
        in_specs=(P("blk", None), P(None, "blk", "grp"), P()),
        out_specs=P(("blk", "grp"), None),
        check_vma=False,
    )
```

```python
import functools

import jax
import jax.numpy as jnp
from jax import lax
from jax.experimental import pallas as pl
from jax.experimental.pallas import tpu as pltpu
from jax.sharding import PartitionSpec as P

TILE = 256
PLANES = 8
WORDS = TILE // PLANES
SECTIONS = 4
LINE = 8

ANYWHERE = pl.BlockSpec(memory_space=pltpu.HBM)
SCALARS = pl.BlockSpec(memory_space=pltpu.SMEM)
VECTORS = pl.BlockSpec(memory_space=pltpu.VMEM)


def local_call(kernel, outs, ins, scratch=(), cost=None, limit=32 << 20):
    return pl.pallas_call(
        kernel,
        out_shape=outs,
        in_specs=ins,
        out_specs=jax.tree.map(lambda _: VECTORS, outs),
        scratch_shapes=scratch,
        cost_estimate=cost,
        compiler_params=pltpu.CompilerParams(vmem_limit_bytes=limit),
    )


def own_kernel(owners_ref, emb_ref, own_ref, list_ref, held_ref, sem):
    blocks, deep, lanes = own_ref.shape
    quarter, width = held_ref.shape
    start = lax.axis_index("grp") * quarter
    rows = pl.ds(pl.multiple_of(start, quarter), quarter)
    copy = pltpu.make_async_copy(emb_ref.at[rows, :], held_ref, sem.at[0])
    names = pltpu.make_async_copy(owners_ref, list_ref, sem.at[1])
    copy.start()
    names.start()
    copy.wait()
    chunks = quarter // deep
    for part in range(width // lanes):
        for chunk in range(chunks):
            own_ref[part * chunks + chunk] = held_ref[
                chunk * deep : (chunk + 1) * deep, part * lanes : (part + 1) * lanes
            ]
    names.wait()


def to_line_kernel(owners_ref, got_ref, sent_ref):
    for s in range(SECTIONS):
        held = got_ref[owners_ref[s]]
        for part in range(sent_ref.shape[0]):
            sent_ref[part, s] = held


def to_plane_kernel(came_ref, sent_ref):
    held = came_ref[...]
    for part in range(sent_ref.shape[0]):
        sent_ref[part] = held


def products_kernel(
    emb_ref, pieces_ref, far_words_ref, keep_ref, send_ref, col_ref,
    block_ref, halved_ref, rows_ref, cols_ref, error_ref, words_ref, sem,
):
    plane, line, sections, deep, lanes = pieces_ref.shape
    rows, width = emb_ref.shape
    fetch = pltpu.make_async_copy(far_words_ref, words_ref, sem)
    fetch.start()
    quarter = rows // 4
    place = lax.axis_index("grp")
    core, high = place % 2, place // 2
    for section in range(sections):
        for z in range(line):
            for xy in range(plane):
                at = section * quarter + (z * 4 + xy % 4) * deep
                span = slice(at, at + deep)
                cut = slice(xy // 4 * lanes, (xy // 4 + 1) * lanes)
                value = pieces_ref[xy, z, section]
                block_ref[span, cut] = value
                halved_ref[span, cut] = value * jnp.bfloat16(0.5)

    new = lax.broadcasted_iota(jnp.int32, (TILE, TILE), 0)
    old = lax.broadcasted_iota(jnp.int32, (TILE, TILE), 1)
    pick = old == (new % WORDS) * PLANES + new // WORDS
    order = jnp.where(pick, 1.0, 0.0).astype(jnp.bfloat16)
    source = (new // 128) * 128 + (new // 4 % 8) * 16 + (new // 32 % 4) * 4 + new % 4
    spread = jnp.where(old == source, 1.0, 0.0).astype(jnp.bfloat16)

    tiles = []
    for away in (1, 0):
        for other in (0, 1):
            for sub in range(2):
                tiles.append(((high ^ away) * 2 + (core ^ other)) * 2 + sub)
    for step, tile in enumerate(tiles):
        span = slice(step * TILE, (step + 1) * TILE)
        raw = emb_ref[pl.ds(pl.multiple_of(tile * TILE, TILE), TILE), :]
        here = jnp.dot(order, raw, preferred_element_type=jnp.float32).astype(jnp.bfloat16)
        rows_ref[span, :] = here
        cols_ref[:, span] = lax.dot_general(
            spread, here, (((1,), (1,)), ((), ())), preferred_element_type=jnp.float32
        ).astype(jnp.bfloat16)
    fetch.wait()
    for pair in range(4):
        span = slice(pair * 2 * TILE, (pair + 1) * 2 * TILE)
        for section in range(sections):
            cut = slice(section * quarter, (section + 1) * quarter)
            scores = lax.dot_general(
                rows_ref[span, :], halved_ref[cut, :], (((1,), (1,)), ((), ())), preferred_element_type=jnp.float32
            )
            for sub in range(2):
                tile = tiles[pair * 2 + sub]
                words = words_ref[section, pl.ds(pl.multiple_of(tile * WORDS, WORDS), WORDS), :]
                for plane in range(PLANES):
                    at = sub * TILE + plane * WORDS
                    sign = jnp.where((words & (1 << plane)) == 0, 1.0, -1.0)
                    error = jnp.tanh(scores[at : at + WORDS, :]) + sign
                    error_ref[pair * 2 * TILE + at : pair * 2 * TILE + at + WORDS, cut] = error.astype(jnp.bfloat16)
        row = jnp.dot(error_ref[span, :], block_ref[...], preferred_element_type=jnp.float32)
        store = keep_ref if pair // 2 else send_ref
        store[pair % 2] = row
    for section in range(sections):
        cut = slice(section * quarter, (section + 1) * quarter)
        col_ref[:, cut] = jnp.dot(cols_ref[...], error_ref[:, cut], preferred_element_type=jnp.float32)


def plane_total(came_ref):
    total = came_ref[0]
    for part in range(1, came_ref.shape[0]):
        total = total + came_ref[part]
    return total


def to_line_sum_kernel(came_ref, out_ref):
    total = plane_total(came_ref)
    deep = out_ref.shape[1]
    for part in range(out_ref.shape[0]):
        out_ref[part] = total[part * deep : (part + 1) * deep, :]


def to_owner_kernel(owners_ref, came_ref, out_ref):
    total = plane_total(came_ref)
    out_ref[...] = jnp.zeros_like(out_ref)
    quarter = out_ref.shape[2]
    for s in range(SECTIONS):
        out_ref[owners_ref[s]] = total[:, s * quarter : (s + 1) * quarter] * 0.125


def finish_kernel(scale, owners_ref, keep_ref, came_ref, back_ref, out_ref, row_ref):
    mine = lax.axis_index("blk")
    owned = jnp.bool_(False)
    for s in range(SECTIONS):
        owned = owned | (owners_ref[s] == mine)
    quarter, width = out_ref.shape
    row = keep_ref[0] + came_ref[...].astype(jnp.float32)
    for tile in range(quarter // TILE):
        for plane in range(PLANES):
            at = tile * TILE + plane * WORDS
            for lane in range(width // 128):
                row_ref[lane, pl.ds(tile * TILE + plane, WORDS, stride=PLANES), :] = row[
                    at : at + WORDS, lane * 128 : (lane + 1) * 128
                ]
    for lane in range(width // 128):
        out_ref[:, lane * 128 : (lane + 1) * 128] = row_ref[lane] * scale

    @pl.when(owned)
    def _():
        out_ref[...] += back_ref[...].reshape(width, quarter).T * (8.0 * scale)


def body(embedding, adjacency, owners):
    rows, width = embedding.shape
    sections = adjacency.shape[0]
    groups = lax.axis_size("grp")
    blocks = lax.axis_size("blk")
    quarter = rows // groups
    wide = sections * quarter
    plane_xy = [[x * 32 + z * 4 + y for x in range(2) for y in range(4)] for z in range(LINE)]
    line_z = [[x * 32 + z * 4 + y for z in range(LINE)] for x in range(2) for y in range(4)]

    fence = lax.optimization_barrier

    def swap(value, line=None):
        return lax.all_to_all(value, "blk", 0, 0, axis_index_groups=line)

    def shape(*extent, dtype=jnp.float32):
        return jax.ShapeDtypeStruct(extent, dtype)

    half = jnp.bfloat16
    deep, lanes = 2 * quarter // blocks, width // 2
    own, owners = local_call(
        own_kernel,
        (shape(blocks, deep, lanes, dtype=half), shape(blocks, dtype=jnp.int32)),
        [ANYWHERE, ANYWHERE],
        [pltpu.VMEM((quarter, width), half), pltpu.SemaphoreType.DMA((2,))],
    )(owners, embedding)
    got = swap(own)
    sent = local_call(to_line_kernel, shape(LINE, sections, deep, lanes, dtype=half), [SCALARS, VECTORS])(owners, got)
    came = swap(sent, line_z)
    spread = local_call(to_plane_kernel, shape(LINE, LINE, sections, deep, lanes, dtype=half), [VECTORS])(came)
    pieces = swap(spread, plane_xy)

    keep, send, col = local_call(
        products_kernel,
        (shape(2, quarter, width), shape(2, quarter, width), shape(width, wide)),
        [VECTORS, VECTORS, ANYWHERE],
        [
            pltpu.VMEM((wide, width), half),
            pltpu.VMEM((wide, width), half),
            pltpu.VMEM((rows, width), half),
            pltpu.VMEM((width, rows), half),
            pltpu.VMEM((rows, wide), half),
            pltpu.VMEM(adjacency.shape, jnp.int32),
            pltpu.SemaphoreType.DMA,
        ],
        pl.CostEstimate(flops=6 * rows * wide * width, bytes_accessed=9 << 20, transcendentals=rows * wide),
    )(embedding, pieces, adjacency)

    col = col.astype(jnp.float16).reshape(LINE, width // LINE, wide)
    col = fence(swap(fence(col), plane_xy))
    col, keep, send = fence((col.astype(jnp.float32), keep, send))
    col = local_call(to_line_sum_kernel, shape(LINE, width // blocks, wide), [VECTORS])(col)
    far = lax.ppermute(send.astype(jnp.float16), "grp", [(g, g ^ 2) for g in range(groups)])
    col = swap(col.astype(jnp.float16), line_z).astype(jnp.float32)
    col, far, keep = fence((col, far, keep))
    keep = keep + far.astype(jnp.float32)
    col = local_call(to_owner_kernel, shape(blocks, width // blocks, quarter), [SCALARS, VECTORS])(owners, col)
    far = lax.ppermute(keep[1].astype(jnp.float16), "grp", [(g, g ^ 1) for g in range(groups)]).astype(jnp.float32)
    back = swap(col.astype(jnp.float16)).astype(jnp.float32)
    return local_call(
        functools.partial(finish_kernel, 0.5 * rows ** (-0.5)),
        shape(quarter, width),
        [SCALARS, VECTORS, VECTORS, VECTORS],
        [pltpu.VMEM((width // 128, quarter, 128), jnp.float32)],
    )(owners, keep, far, back)


def solution(mesh):
    return jax.shard_map(
        body,
        mesh=mesh,
        in_specs=(P("blk", None), P(None, "blk", "grp"), P()),
        out_specs=P(("blk", "grp"), None),
        check_vma=False,
    )
```

```python
import functools

import jax
import jax.numpy as jnp
from jax import lax
from jax.experimental import pallas as pl
from jax.experimental.pallas import tpu as pltpu
from jax.sharding import PartitionSpec as P

TILE = 256
PLANES = 8
WORDS = TILE // PLANES
SECTIONS = 4
LINE = 8

ANYWHERE = pl.BlockSpec(memory_space=pltpu.HBM)
SCALARS = pl.BlockSpec(memory_space=pltpu.SMEM)
VECTORS = pl.BlockSpec(memory_space=pltpu.VMEM)


def local_call(kernel, outs, ins, scratch=(), cost=None, limit=32 << 20):
    return pl.pallas_call(
        kernel,
        out_shape=outs,
        in_specs=ins,
        out_specs=jax.tree.map(lambda _: VECTORS, outs),
        scratch_shapes=scratch,
        cost_estimate=cost,
        compiler_params=pltpu.CompilerParams(vmem_limit_bytes=limit),
    )


def own_kernel(owners_ref, emb_ref, own_ref, list_ref, held_ref, sem):
    blocks, deep, lanes = own_ref.shape
    quarter, width = held_ref.shape
    start = lax.axis_index("grp") * quarter
    rows = pl.ds(pl.multiple_of(start, quarter), quarter)
    copy = pltpu.make_async_copy(emb_ref.at[rows, :], held_ref, sem.at[0])
    names = pltpu.make_async_copy(owners_ref, list_ref, sem.at[1])
    copy.start()
    names.start()
    copy.wait()
    chunks = quarter // deep
    for part in range(width // lanes):
        for chunk in range(chunks):
            own_ref[part * chunks + chunk] = held_ref[
                chunk * deep : (chunk + 1) * deep, part * lanes : (part + 1) * lanes
            ]
    names.wait()


def to_line_kernel(owners_ref, got_ref, sent_ref):
    for s in range(SECTIONS):
        held = got_ref[owners_ref[s]]
        for part in range(sent_ref.shape[0]):
            sent_ref[part, s] = held


def to_plane_kernel(came_ref, sent_ref):
    held = came_ref[...]
    for part in range(sent_ref.shape[0]):
        sent_ref[part] = held


def products_kernel(
    emb_ref, pieces_ref, words_ref, keep_ref, send_ref, col_ref,
    block_ref, rows_ref, cols_ref, error_ref,
):
    plane, line, sections, deep, lanes = pieces_ref.shape
    rows, width = emb_ref.shape
    quarter = rows // 4
    place = lax.axis_index("grp")
    core, high = place % 2, place // 2
    for section in range(sections):
        for z in range(line):
            for xy in range(plane):
                at = section * quarter + (z * 4 + xy % 4) * deep
                span = slice(at, at + deep)
                cut = slice(xy // 4 * lanes, (xy // 4 + 1) * lanes)
                block_ref[span, cut] = pieces_ref[xy, z, section]

    new = lax.broadcasted_iota(jnp.int32, (TILE, TILE), 0)
    old = lax.broadcasted_iota(jnp.int32, (TILE, TILE), 1)
    pick = old == (new % WORDS) * PLANES + new // WORDS
    order = jnp.where(pick, 0.5, 0.0).astype(jnp.bfloat16)
    source = (new // 128) * 128 + (new // 4 % 8) * 16 + (new // 32 % 4) * 4 + new % 4
    spread = jnp.where(old == source, 2.0, 0.0).astype(jnp.bfloat16)

    tiles = []
    for away in (1, 0):
        for other in (0, 1):
            for sub in range(2):
                tiles.append(((high ^ away) * 2 + (core ^ other)) * 2 + sub)
    for step, tile in enumerate(tiles):
        span = slice(step * TILE, (step + 1) * TILE)
        raw = emb_ref[pl.ds(pl.multiple_of(tile * TILE, TILE), TILE), :]
        here = jnp.dot(order, raw, preferred_element_type=jnp.float32).astype(jnp.bfloat16)
        rows_ref[span, :] = here
        cols_ref[:, span] = lax.dot_general(
            spread, here, (((1,), (1,)), ((), ())), preferred_element_type=jnp.float32
        ).astype(jnp.bfloat16)
    for pair in range(4):
        span = slice(pair * 2 * TILE, (pair + 1) * 2 * TILE)
        for section in range(sections):
            cut = slice(section * quarter, (section + 1) * quarter)
            scores = lax.dot_general(
                rows_ref[span, :], block_ref[cut, :], (((1,), (1,)), ((), ())), preferred_element_type=jnp.float32
            )
            for sub in range(2):
                tile = tiles[pair * 2 + sub]
                words = words_ref[section, pl.ds(pl.multiple_of(tile * WORDS, WORDS), WORDS), :]
                for plane in range(PLANES):
                    at = sub * TILE + plane * WORDS
                    sign = jnp.where((words & (1 << plane)) == 0, 1.0, -1.0)
                    error = jnp.tanh(scores[at : at + WORDS, :]) + sign
                    error_ref[pair * 2 * TILE + at : pair * 2 * TILE + at + WORDS, cut] = error.astype(jnp.bfloat16)
        row = jnp.dot(error_ref[span, :], block_ref[...], preferred_element_type=jnp.float32)
        store = keep_ref if pair // 2 else send_ref
        store[pair % 2] = row
    for section in range(sections):
        cut = slice(section * quarter, (section + 1) * quarter)
        col_ref[:, cut] = jnp.dot(cols_ref[...], error_ref[:, cut], preferred_element_type=jnp.float32)


def plane_total(came_ref):
    total = came_ref[0]
    for part in range(1, came_ref.shape[0]):
        total = total + came_ref[part]
    return total


def to_line_sum_kernel(came_ref, out_ref):
    total = plane_total(came_ref)
    deep = out_ref.shape[1]
    for part in range(out_ref.shape[0]):
        out_ref[part] = total[part * deep : (part + 1) * deep, :]


def to_owner_kernel(owners_ref, came_ref, out_ref):
    total = plane_total(came_ref)
    out_ref[...] = jnp.zeros_like(out_ref)
    quarter = out_ref.shape[2]
    for s in range(SECTIONS):
        out_ref[owners_ref[s]] = total[:, s * quarter : (s + 1) * quarter] * 0.125


def finish_kernel(scale, owners_ref, keep_ref, came_ref, back_ref, out_ref, row_ref):
    mine = lax.axis_index("blk")
    owned = jnp.bool_(False)
    for s in range(SECTIONS):
        owned = owned | (owners_ref[s] == mine)
    quarter, width = out_ref.shape
    row = keep_ref[0] + came_ref[...].astype(jnp.float32)
    for tile in range(quarter // TILE):
        for plane in range(PLANES):
            at = tile * TILE + plane * WORDS
            for lane in range(width // 128):
                row_ref[lane, pl.ds(tile * TILE + plane, WORDS, stride=PLANES), :] = row[
                    at : at + WORDS, lane * 128 : (lane + 1) * 128
                ]
    for lane in range(width // 128):
        out_ref[:, lane * 128 : (lane + 1) * 128] = row_ref[lane] * scale

    @pl.when(owned)
    def _():
        out_ref[...] += back_ref[...].reshape(width, quarter).T * (8.0 * scale)


def body(embedding, adjacency, owners):
    rows, width = embedding.shape
    sections = adjacency.shape[0]
    groups = lax.axis_size("grp")
    blocks = lax.axis_size("blk")
    quarter = rows // groups
    wide = sections * quarter
    plane_xy = [[x * 32 + z * 4 + y for x in range(2) for y in range(4)] for z in range(LINE)]
    line_z = [[x * 32 + z * 4 + y for z in range(LINE)] for x in range(2) for y in range(4)]

    fence = lax.optimization_barrier

    def swap(value, line=None):
        return lax.all_to_all(value, "blk", 0, 0, axis_index_groups=line)

    def shape(*extent, dtype=jnp.float32):
        return jax.ShapeDtypeStruct(extent, dtype)

    half = jnp.bfloat16
    deep, lanes = 2 * quarter // blocks, width // 2
    own, owners = local_call(
        own_kernel,
        (shape(blocks, deep, lanes, dtype=half), shape(blocks, dtype=jnp.int32)),
        [ANYWHERE, ANYWHERE],
        [pltpu.VMEM((quarter, width), half), pltpu.SemaphoreType.DMA((2,))],
    )(owners, embedding)
    got = swap(own)
    sent = local_call(to_line_kernel, shape(LINE, sections, deep, lanes, dtype=half), [SCALARS, VECTORS])(owners, got)
    came = swap(sent, line_z)
    spread = local_call(to_plane_kernel, shape(LINE, LINE, sections, deep, lanes, dtype=half), [VECTORS])(came)
    pieces = swap(spread, plane_xy)

    keep, send, col = local_call(
        products_kernel,
        (shape(2, quarter, width), shape(2, quarter, width), shape(width, wide)),
        [VECTORS] * 3,
        [
            pltpu.VMEM((wide, width), half),
            pltpu.VMEM((rows, width), half),
            pltpu.VMEM((width, rows), half),
            pltpu.VMEM((rows, wide), half),
        ],
        pl.CostEstimate(flops=6 * rows * wide * width, bytes_accessed=9 << 20, transcendentals=rows * wide),
    )(embedding, pieces, adjacency)

    col = col.astype(jnp.float16).reshape(LINE, width // LINE, wide)
    col = fence(swap(fence(col), plane_xy))
    col, keep, send = fence((col.astype(jnp.float32), keep, send))
    col = local_call(to_line_sum_kernel, shape(LINE, width // blocks, wide), [VECTORS])(col)
    far = lax.ppermute(send.astype(jnp.float16), "grp", [(g, g ^ 2) for g in range(groups)])
    col = swap(col.astype(jnp.float16), line_z).astype(jnp.float32)
    col, far, keep = fence((col, far, keep))
    keep = keep + far.astype(jnp.float32)
    col = local_call(to_owner_kernel, shape(blocks, width // blocks, quarter), [SCALARS, VECTORS])(owners, col)
    far = lax.ppermute(keep[1].astype(jnp.float16), "grp", [(g, g ^ 1) for g in range(groups)]).astype(jnp.float32)
    back = swap(col.astype(jnp.float16)).astype(jnp.float32)
    return local_call(
        functools.partial(finish_kernel, 0.5 * rows ** (-0.5)),
        shape(quarter, width),
        [SCALARS, VECTORS, VECTORS, VECTORS],
        [pltpu.VMEM((width // 128, quarter, 128), jnp.float32)],
    )(owners, keep, far, back)


def solution(mesh):
    return jax.shard_map(
        body,
        mesh=mesh,
        in_specs=(P("blk", None), P(None, "blk", "grp"), P()),
        out_specs=P(("blk", "grp"), None),
        check_vma=False,
    )
```

```python
import functools

import jax
import jax.numpy as jnp
from jax import lax
from jax.experimental import pallas as pl
from jax.experimental.pallas import tpu as pltpu
from jax.sharding import PartitionSpec as P

TILE = 256
PLANES = 8
WORDS = TILE // PLANES
SECTIONS = 4
LINE = 8

ANYWHERE = pl.BlockSpec(memory_space=pltpu.HBM)
SCALARS = pl.BlockSpec(memory_space=pltpu.SMEM)
VECTORS = pl.BlockSpec(memory_space=pltpu.VMEM)


def local_call(kernel, outs, ins, scratch=(), cost=None, limit=32 << 20):
    return pl.pallas_call(
        kernel,
        out_shape=outs,
        in_specs=ins,
        out_specs=jax.tree.map(lambda _: VECTORS, outs),
        scratch_shapes=scratch,
        cost_estimate=cost,
        compiler_params=pltpu.CompilerParams(vmem_limit_bytes=limit),
    )


def own_kernel(owners_ref, emb_ref, own_ref, list_ref, held_ref, sem):
    blocks, deep, lanes = own_ref.shape
    quarter, width = held_ref.shape
    start = lax.axis_index("grp") * quarter
    rows = pl.ds(pl.multiple_of(start, quarter), quarter)
    copy = pltpu.make_async_copy(emb_ref.at[rows, :], held_ref, sem.at[0])
    names = pltpu.make_async_copy(owners_ref, list_ref, sem.at[1])
    copy.start()
    names.start()
    copy.wait()
    chunks = quarter // deep
    for part in range(width // lanes):
        for chunk in range(chunks):
            own_ref[part * chunks + chunk] = held_ref[
                chunk * deep : (chunk + 1) * deep, part * lanes : (part + 1) * lanes
            ]
    names.wait()


def to_line_kernel(owners_ref, got_ref, sent_ref):
    for s in range(SECTIONS):
        held = got_ref[owners_ref[s]]
        for part in range(sent_ref.shape[0]):
            sent_ref[part, s] = held


def to_plane_kernel(came_ref, sent_ref):
    held = came_ref[...]
    for part in range(sent_ref.shape[0]):
        sent_ref[part] = held


def products_kernel(
    emb_ref, pieces_ref, words_ref, keep_ref, send_ref, col_ref,
    block_ref, rows_ref, cols_ref, error_ref,
):
    plane, line, sections, deep, lanes = pieces_ref.shape
    rows, width = emb_ref.shape
    quarter = rows // 4
    place = lax.axis_index("grp")
    core, high = place % 2, place // 2
    for section in range(sections):
        for z in range(line):
            for xy in range(plane):
                at = section * quarter + (z * 4 + xy % 4) * deep
                span = slice(at, at + deep)
                cut = slice(xy // 4 * lanes, (xy // 4 + 1) * lanes)
                block_ref[span, cut] = pieces_ref[xy, z, section]

    new = lax.broadcasted_iota(jnp.int32, (TILE, TILE), 0)
    old = lax.broadcasted_iota(jnp.int32, (TILE, TILE), 1)
    pick = old == (new % WORDS) * PLANES + new // WORDS
    order = jnp.where(pick, 0.5, 0.0).astype(jnp.bfloat16)
    source = (new // 128) * 128 + (new // 4 % 8) * 16 + (new // 32 % 4) * 4 + new % 4
    spread = jnp.where(old == source, 2.0, 0.0).astype(jnp.bfloat16)

    tiles = []
    for away in (1, 0):
        for other in (0, 1):
            for sub in range(2):
                tiles.append(((high ^ away) * 2 + (core ^ other)) * 2 + sub)
    for step, tile in enumerate(tiles):
        span = slice(step * TILE, (step + 1) * TILE)
        raw = emb_ref[pl.ds(pl.multiple_of(tile * TILE, TILE), TILE), :]
        here = jnp.dot(order, raw, preferred_element_type=jnp.float32).astype(jnp.bfloat16)
        rows_ref[span, :] = here
        cols_ref[:, span] = lax.dot_general(
            spread, here, (((1,), (1,)), ((), ())), preferred_element_type=jnp.float32
        ).astype(jnp.bfloat16)
    for pair in range(4):
        span = slice(pair * 2 * TILE, (pair + 1) * 2 * TILE)
        for section in range(sections):
            cut = slice(section * quarter, (section + 1) * quarter)
            scores = lax.dot_general(
                rows_ref[span, :], block_ref[cut, :], (((1,), (1,)), ((), ())), preferred_element_type=jnp.float32
            )
            for sub in range(2):
                tile = tiles[pair * 2 + sub]
                words = words_ref[section, pl.ds(pl.multiple_of(tile * WORDS, WORDS), WORDS), :]
                for plane in range(PLANES):
                    at = sub * TILE + plane * WORDS
                    sign = jnp.where((words & (1 << plane)) == 0, 1.0, -1.0)
                    error = jnp.tanh(scores[at : at + WORDS, :]) + sign
                    error_ref[pair * 2 * TILE + at : pair * 2 * TILE + at + WORDS, cut] = error.astype(jnp.bfloat16)
        row = jnp.dot(error_ref[span, :], block_ref[...], preferred_element_type=jnp.float32)
        store = keep_ref if pair // 2 else send_ref
        store[pair % 2] = row
    for section in range(sections):
        cut = slice(section * quarter, (section + 1) * quarter)
        col_ref[:, cut] = jnp.dot(cols_ref[...], error_ref[:, cut], preferred_element_type=jnp.float32)


def plane_total(came_ref):
    total = came_ref[0]
    for part in range(1, came_ref.shape[0]):
        total = total + came_ref[part]
    return total


def to_line_sum_kernel(came_ref, out_ref):
    total = plane_total(came_ref)
    deep = out_ref.shape[1]
    for part in range(out_ref.shape[0]):
        out_ref[part] = total[part * deep : (part + 1) * deep, :]


def to_owner_kernel(owners_ref, came_ref, out_ref):
    total = plane_total(came_ref)
    out_ref[...] = jnp.zeros_like(out_ref)
    quarter = out_ref.shape[2]
    for s in range(SECTIONS):
        out_ref[owners_ref[s]] = total[:, s * quarter : (s + 1) * quarter] * 0.125


def finish_kernel(scale, owners_ref, keep_ref, came_ref, back_ref, out_ref, row_ref):
    mine = lax.axis_index("blk")
    owned = jnp.bool_(False)
    for s in range(SECTIONS):
        owned = owned | (owners_ref[s] == mine)
    quarter, width = out_ref.shape
    row = keep_ref[0] + came_ref[...].astype(jnp.float32)
    for tile in range(quarter // TILE):
        for plane in range(PLANES):
            at = tile * TILE + plane * WORDS
            for lane in range(width // 128):
                row_ref[lane, pl.ds(tile * TILE + plane, WORDS, stride=PLANES), :] = row[
                    at : at + WORDS, lane * 128 : (lane + 1) * 128
                ]
    for lane in range(width // 128):
        out_ref[:, lane * 128 : (lane + 1) * 128] = row_ref[lane, :quarter, :] * scale

    @pl.when(owned)
    def _():
        out_ref[...] += back_ref[...].reshape(width, quarter).T * (8.0 * scale)


def body(embedding, adjacency, owners):
    rows, width = embedding.shape
    sections = adjacency.shape[0]
    groups = lax.axis_size("grp")
    blocks = lax.axis_size("blk")
    quarter = rows // groups
    wide = sections * quarter
    plane_xy = [[x * 32 + z * 4 + y for x in range(2) for y in range(4)] for z in range(LINE)]
    line_z = [[x * 32 + z * 4 + y for z in range(LINE)] for x in range(2) for y in range(4)]

    fence = lax.optimization_barrier

    def swap(value, line=None):
        return lax.all_to_all(value, "blk", 0, 0, axis_index_groups=line)

    def shape(*extent, dtype=jnp.float32):
        return jax.ShapeDtypeStruct(extent, dtype)

    half = jnp.bfloat16
    deep, lanes = 2 * quarter // blocks, width // 2
    own, owners = local_call(
        own_kernel,
        (shape(blocks, deep, lanes, dtype=half), shape(blocks, dtype=jnp.int32)),
        [ANYWHERE, ANYWHERE],
        [pltpu.VMEM((quarter, width), half), pltpu.SemaphoreType.DMA((2,))],
    )(owners, embedding)
    got = swap(own)
    sent = local_call(to_line_kernel, shape(LINE, sections, deep, lanes, dtype=half), [SCALARS, VECTORS])(owners, got)
    came = swap(sent, line_z)
    spread = local_call(to_plane_kernel, shape(LINE, LINE, sections, deep, lanes, dtype=half), [VECTORS])(came)
    pieces = swap(spread, plane_xy)

    keep, send, col = local_call(
        products_kernel,
        (shape(2, quarter, width), shape(2, quarter, width), shape(width, wide)),
        [VECTORS] * 3,
        [
            pltpu.VMEM((wide, width), half),
            pltpu.VMEM((rows, width), half),
            pltpu.VMEM((width, rows), half),
            pltpu.VMEM((rows, wide), half),
        ],
        pl.CostEstimate(flops=6 * rows * wide * width, bytes_accessed=9 << 20, transcendentals=rows * wide),
    )(embedding, pieces, adjacency)

    col = col.astype(jnp.float16).reshape(LINE, width // LINE, wide)
    col = fence(swap(fence(col), plane_xy))
    col, keep, send = fence((col.astype(jnp.float32), keep, send))
    col = local_call(to_line_sum_kernel, shape(LINE, width // blocks, wide), [VECTORS])(col)
    far = lax.ppermute(send.astype(jnp.float16), "grp", [(g, g ^ 2) for g in range(groups)])
    col = swap(col.astype(jnp.float16), line_z).astype(jnp.float32)
    col, far, keep = fence((col, far, keep))
    keep = keep + far.astype(jnp.float32)
    col = local_call(to_owner_kernel, shape(blocks, width // blocks, quarter), [SCALARS, VECTORS])(owners, col)
    far = lax.ppermute(keep[1].astype(jnp.float16), "grp", [(g, g ^ 1) for g in range(groups)]).astype(jnp.float32)
    back = swap(col.astype(jnp.float16)).astype(jnp.float32)
    return local_call(
        functools.partial(finish_kernel, 0.5 * rows ** (-0.5)),
        shape(quarter, width),
        [SCALARS, VECTORS, VECTORS, VECTORS],
        [pltpu.VMEM((width // 128, quarter + PLANES, 128), jnp.float32)],
    )(owners, keep, far, back)


def solution(mesh):
    return jax.shard_map(
        body,
        mesh=mesh,
        in_specs=(P("blk", None), P(None, "blk", "grp"), P()),
        out_specs=P(("blk", "grp"), None),
        check_vma=False,
    )
```

```python
import functools

import jax
import jax.numpy as jnp
from jax import lax
from jax.experimental import pallas as pl
from jax.experimental.pallas import tpu as pltpu
from jax.sharding import PartitionSpec as P

TILE = 256
PLANES = 8
WORDS = TILE // PLANES
SECTIONS = 4
LINE = 8

ANYWHERE = pl.BlockSpec(memory_space=pltpu.HBM)
SCALARS = pl.BlockSpec(memory_space=pltpu.SMEM)
VECTORS = pl.BlockSpec(memory_space=pltpu.VMEM)


def local_call(kernel, outs, ins, scratch=(), cost=None, limit=32 << 20):
    return pl.pallas_call(
        kernel,
        out_shape=outs,
        in_specs=ins,
        out_specs=jax.tree.map(lambda _: VECTORS, outs),
        scratch_shapes=scratch,
        cost_estimate=cost,
        compiler_params=pltpu.CompilerParams(vmem_limit_bytes=limit),
    )


def own_kernel(owners_ref, emb_ref, own_ref, list_ref, held_ref, sem):
    blocks, deep, lanes = own_ref.shape
    quarter, width = held_ref.shape
    start = lax.axis_index("grp") * quarter
    rows = pl.ds(pl.multiple_of(start, quarter), quarter)
    copy = pltpu.make_async_copy(emb_ref.at[rows, :], held_ref, sem.at[0])
    names = pltpu.make_async_copy(owners_ref, list_ref, sem.at[1])
    copy.start()
    names.start()
    copy.wait()
    chunks = quarter // deep
    for part in range(width // lanes):
        for chunk in range(chunks):
            own_ref[part * chunks + chunk] = held_ref[
                chunk * deep : (chunk + 1) * deep, part * lanes : (part + 1) * lanes
            ]
    names.wait()


def to_line_kernel(owners_ref, got_ref, sent_ref):
    for s in range(SECTIONS):
        held = got_ref[owners_ref[s]]
        for part in range(sent_ref.shape[0]):
            sent_ref[part, s] = held


def to_plane_kernel(came_ref, sent_ref):
    held = came_ref[...]
    for part in range(sent_ref.shape[0]):
        sent_ref[part] = held


def products_kernel(
    emb_ref, pieces_ref, words_ref, keep_ref, send_ref, col_ref,
    block_ref, rows_ref, cols_ref, error_ref,
):
    plane, line, sections, deep, lanes = pieces_ref.shape
    rows, width = emb_ref.shape
    quarter = rows // 4
    place = lax.axis_index("grp")
    core, high = place % 2, place // 2
    for section in range(sections):
        for z in range(line):
            for xy in range(plane):
                at = section * quarter + (z * 4 + xy % 4) * deep
                span = slice(at, at + deep)
                cut = slice(xy // 4 * lanes, (xy // 4 + 1) * lanes)
                block_ref[span, cut] = pieces_ref[xy, z, section]

    new = lax.broadcasted_iota(jnp.int32, (TILE, TILE), 0)
    old = lax.broadcasted_iota(jnp.int32, (TILE, TILE), 1)
    pick = old == (new % WORDS) * PLANES + new // WORDS
    order = jnp.where(pick, 0.5, 0.0).astype(jnp.bfloat16)
    source = (new // 128) * 128 + (new // 4 % 8) * 16 + (new // 32 % 4) * 4 + new % 4
    spread = jnp.where(old == source, 2.0, 0.0).astype(jnp.bfloat16)

    tiles = []
    for away in (1, 0):
        for other in (0, 1):
            for sub in range(2):
                tiles.append(((high ^ away) * 2 + (core ^ other)) * 2 + sub)
    for step, tile in enumerate(tiles):
        span = slice(step * TILE, (step + 1) * TILE)
        raw = emb_ref[pl.ds(pl.multiple_of(tile * TILE, TILE), TILE), :]
        here = jnp.dot(order, raw, preferred_element_type=jnp.float32).astype(jnp.bfloat16)
        rows_ref[span, :] = here
        cols_ref[:, span] = lax.dot_general(
            spread, here, (((1,), (1,)), ((), ())), preferred_element_type=jnp.float32
        ).astype(jnp.bfloat16)
    for pair in range(4):
        span = slice(pair * 2 * TILE, (pair + 1) * 2 * TILE)
        for section in range(sections):
            cut = slice(section * quarter, (section + 1) * quarter)
            scores = lax.dot_general(
                rows_ref[span, :], block_ref[cut, :], (((1,), (1,)), ((), ())), preferred_element_type=jnp.float32
            )
            for sub in range(2):
                tile = tiles[pair * 2 + sub]
                words = words_ref[section, pl.ds(pl.multiple_of(tile * WORDS, WORDS), WORDS), :]
                for plane in range(PLANES):
                    at = sub * TILE + plane * WORDS
                    sign = jnp.where((words & (1 << plane)) == 0, 1.0, -1.0)
                    error = jnp.tanh(scores[at : at + WORDS, :]) + sign
                    error_ref[pair * 2 * TILE + at : pair * 2 * TILE + at + WORDS, cut] = error.astype(jnp.bfloat16)
        row = jnp.dot(error_ref[span, :], block_ref[...], preferred_element_type=jnp.float32)
        store = keep_ref if pair // 2 else send_ref
        store[pair % 2] = row
    for section in range(sections):
        cut = slice(section * quarter, (section + 1) * quarter)
        col_ref[:, cut] = jnp.dot(cols_ref[...], error_ref[:, cut], preferred_element_type=jnp.float32)


def plane_total(came_ref):
    total = came_ref[0]
    for part in range(1, came_ref.shape[0]):
        total = total + came_ref[part]
    return total


def to_line_sum_kernel(came_ref, out_ref):
    total = plane_total(came_ref)
    deep = out_ref.shape[1]
    for part in range(out_ref.shape[0]):
        out_ref[part] = total[part * deep : (part + 1) * deep, :]


def to_owner_kernel(owners_ref, came_ref, out_ref):
    total = plane_total(came_ref)
    out_ref[...] = jnp.zeros_like(out_ref)
    quarter = out_ref.shape[2]
    for s in range(SECTIONS):
        out_ref[owners_ref[s]] = total[:, s * quarter : (s + 1) * quarter] * 0.125


def rows_kernel(scale, keep_ref, came_ref, out_ref, row_ref):
    quarter, width = out_ref.shape
    row = keep_ref[0] + came_ref[...]
    for tile in range(quarter // TILE):
        for plane in range(PLANES):
            at = tile * TILE + plane * WORDS
            for lane in range(width // 128):
                row_ref[lane, pl.ds(tile * TILE + plane, WORDS, stride=PLANES), :] = row[
                    at : at + WORDS, lane * 128 : (lane + 1) * 128
                ]
    for lane in range(width // 128):
        out_ref[:, lane * 128 : (lane + 1) * 128] = row_ref[lane, :quarter, :] * scale


def finish_kernel(scale, owners_ref, rows_ref, back_ref, out_ref):
    mine = lax.axis_index("blk")
    owned = jnp.bool_(False)
    for s in range(SECTIONS):
        owned = owned | (owners_ref[s] == mine)
    quarter, width = out_ref.shape

    @pl.when(owned)
    def _():
        out_ref[...] = rows_ref[...] + back_ref[...].reshape(width, quarter).T * (8.0 * scale)

    @pl.when(jnp.logical_not(owned))
    def _():
        out_ref[...] = rows_ref[...]


def body(embedding, adjacency, owners):
    rows, width = embedding.shape
    sections = adjacency.shape[0]
    groups = lax.axis_size("grp")
    blocks = lax.axis_size("blk")
    quarter = rows // groups
    wide = sections * quarter
    plane_xy = [[x * 32 + z * 4 + y for x in range(2) for y in range(4)] for z in range(LINE)]
    line_z = [[x * 32 + z * 4 + y for z in range(LINE)] for x in range(2) for y in range(4)]

    fence = lax.optimization_barrier

    def swap(value, line=None):
        return lax.all_to_all(value, "blk", 0, 0, axis_index_groups=line)

    def shape(*extent, dtype=jnp.float32):
        return jax.ShapeDtypeStruct(extent, dtype)

    half = jnp.bfloat16
    deep, lanes = 2 * quarter // blocks, width // 2
    own, owners = local_call(
        own_kernel,
        (shape(blocks, deep, lanes, dtype=half), shape(blocks, dtype=jnp.int32)),
        [ANYWHERE, ANYWHERE],
        [pltpu.VMEM((quarter, width), half), pltpu.SemaphoreType.DMA((2,))],
    )(owners, embedding)
    got = swap(own)
    sent = local_call(to_line_kernel, shape(LINE, sections, deep, lanes, dtype=half), [SCALARS, VECTORS])(owners, got)
    came = swap(sent, line_z)
    spread = local_call(to_plane_kernel, shape(LINE, LINE, sections, deep, lanes, dtype=half), [VECTORS])(came)
    pieces = swap(spread, plane_xy)

    keep, send, col = local_call(
        products_kernel,
        (shape(2, quarter, width), shape(2, quarter, width), shape(width, wide)),
        [VECTORS] * 3,
        [
            pltpu.VMEM((wide, width), half),
            pltpu.VMEM((rows, width), half),
            pltpu.VMEM((width, rows), half),
            pltpu.VMEM((rows, wide), half),
        ],
        pl.CostEstimate(flops=6 * rows * wide * width, bytes_accessed=9 << 20, transcendentals=rows * wide),
    )(embedding, pieces, adjacency)

    col = col.astype(jnp.float16).reshape(LINE, width // LINE, wide)
    col = fence(swap(fence(col), plane_xy))
    col, keep, send = fence((col.astype(jnp.float32), keep, send))
    col = local_call(to_line_sum_kernel, shape(LINE, width // blocks, wide), [VECTORS])(col)
    far = lax.ppermute(send.astype(jnp.float16), "grp", [(g, g ^ 2) for g in range(groups)])
    col = swap(col.astype(jnp.float16), line_z).astype(jnp.float32)
    col, far, keep = fence((col, far, keep))
    keep = keep + far.astype(jnp.float32)
    col = local_call(to_owner_kernel, shape(blocks, width // blocks, quarter), [SCALARS, VECTORS])(owners, col)
    far = lax.ppermute(keep[1].astype(jnp.float16), "grp", [(g, g ^ 1) for g in range(groups)]).astype(jnp.float32)
    back = swap(col.astype(jnp.float16)).astype(jnp.float32)
    scale = 0.5 * rows ** (-0.5)
    row = local_call(
        functools.partial(rows_kernel, scale),
        shape(quarter, width),
        [VECTORS] * 2,
        [pltpu.VMEM((width // 128, quarter + PLANES, 128), jnp.float32)],
    )(keep, far)
    return local_call(functools.partial(finish_kernel, scale), shape(quarter, width), [SCALARS, VECTORS, VECTORS])(
        owners, row, back
    )


def solution(mesh):
    return jax.shard_map(
        body,
        mesh=mesh,
        in_specs=(P("blk", None), P(None, "blk", "grp"), P()),
        out_specs=P(("blk", "grp"), None),
        check_vma=False,
    )
```

```python
import functools

import jax
import jax.numpy as jnp
from jax import lax
from jax.experimental import pallas as pl
from jax.experimental.pallas import tpu as pltpu
from jax.sharding import PartitionSpec as P

TILE = 256
PLANES = 8
WORDS = TILE // PLANES
SECTIONS = 4
LINE = 8

ANYWHERE = pl.BlockSpec(memory_space=pltpu.HBM)
SCALARS = pl.BlockSpec(memory_space=pltpu.SMEM)
VECTORS = pl.BlockSpec(memory_space=pltpu.VMEM)


def local_call(kernel, outs, ins, scratch=(), cost=None, limit=32 << 20):
    return pl.pallas_call(
        kernel,
        out_shape=outs,
        in_specs=ins,
        out_specs=jax.tree.map(lambda _: VECTORS, outs),
        scratch_shapes=scratch,
        cost_estimate=cost,
        compiler_params=pltpu.CompilerParams(vmem_limit_bytes=limit),
    )


def own_kernel(owners_ref, emb_ref, own_ref, list_ref, held_ref, sem):
    blocks, deep, lanes = own_ref.shape
    quarter, width = held_ref.shape
    start = lax.axis_index("grp") * quarter
    rows = pl.ds(pl.multiple_of(start, quarter), quarter)
    copy = pltpu.make_async_copy(emb_ref.at[rows, :], held_ref, sem.at[0])
    names = pltpu.make_async_copy(owners_ref, list_ref, sem.at[1])
    copy.start()
    names.start()
    copy.wait()
    chunks = quarter // deep
    for part in range(width // lanes):
        for chunk in range(chunks):
            own_ref[part * chunks + chunk] = held_ref[
                chunk * deep : (chunk + 1) * deep, part * lanes : (part + 1) * lanes
            ]
    names.wait()


def to_line_kernel(owners_ref, got_ref, sent_ref):
    for s in range(SECTIONS):
        held = got_ref[owners_ref[s]]
        for part in range(sent_ref.shape[0]):
            sent_ref[part, s] = held


def to_plane_kernel(came_ref, sent_ref):
    held = came_ref[...]
    for part in range(sent_ref.shape[0]):
        sent_ref[part] = held


def products_kernel(
    emb_ref, pieces_ref, words_ref, keep_ref, send_ref, col_ref,
    block_ref, rows_ref, cols_ref, error_ref,
):
    plane, line, sections, deep, lanes = pieces_ref.shape
    rows, width = emb_ref.shape
    quarter = rows // 4
    place = lax.axis_index("grp")
    core, high = place % 2, place // 2
    for section in range(sections):
        for z in range(line):
            for xy in range(plane):
                at = section * quarter + (z * 4 + xy % 4) * deep
                span = slice(at, at + deep)
                cut = slice(xy // 4 * lanes, (xy // 4 + 1) * lanes)
                block_ref[span, cut] = pieces_ref[xy, z, section]

    new = lax.broadcasted_iota(jnp.int32, (TILE, TILE), 0)
    old = lax.broadcasted_iota(jnp.int32, (TILE, TILE), 1)
    pick = old == (new % WORDS) * PLANES + new // WORDS
    order = jnp.where(pick, 0.5, 0.0).astype(jnp.bfloat16)
    source = (new // 128) * 128 + (new // 4 % 8) * 16 + (new // 32 % 4) * 4 + new % 4
    spread = jnp.where(old == source, 2.0, 0.0).astype(jnp.bfloat16)

    tiles = []
    for away in (1, 0):
        for other in (0, 1):
            for sub in range(2):
                tiles.append(((high ^ away) * 2 + (core ^ other)) * 2 + sub)
    for step, tile in enumerate(tiles):
        span = slice(step * TILE, (step + 1) * TILE)
        raw = emb_ref[pl.ds(pl.multiple_of(tile * TILE, TILE), TILE), :]
        here = jnp.dot(order, raw, preferred_element_type=jnp.float32).astype(jnp.bfloat16)
        rows_ref[span, :] = here
        cols_ref[:, span] = lax.dot_general(
            spread, here, (((1,), (1,)), ((), ())), preferred_element_type=jnp.float32
        ).astype(jnp.bfloat16)

    def scores_of(pair, section):
        return lax.dot_general(
            rows_ref[pair * 2 * TILE : (pair + 1) * 2 * TILE, :],
            block_ref[section * quarter : (section + 1) * quarter, :],
            (((1,), (1,)), ((), ())),
            preferred_element_type=jnp.float32,
        )

    def write_rows(pair):
        span = slice(pair * 2 * TILE, (pair + 1) * 2 * TILE)
        store = keep_ref if pair // 2 else send_ref
        store[pair % 2] = jnp.dot(error_ref[span, :], block_ref[...], preferred_element_type=jnp.float32)

    steps = [(pair, section) for pair in range(4) for section in range(sections)]
    scores = scores_of(*steps[0])
    for step, (pair, section) in enumerate(steps):
        following = scores_of(*steps[step + 1]) if step + 1 < len(steps) else None
        if pair > 0 and section == 0:
            write_rows(pair - 1)
        cut = slice(section * quarter, (section + 1) * quarter)
        for sub in range(2):
            tile = tiles[pair * 2 + sub]
            words = words_ref[section, pl.ds(pl.multiple_of(tile * WORDS, WORDS), WORDS), :]
            for plane in range(PLANES):
                at = sub * TILE + plane * WORDS
                sign = jnp.where((words & (1 << plane)) == 0, 1.0, -1.0)
                error = jnp.tanh(scores[at : at + WORDS, :]) + sign
                error_ref[pair * 2 * TILE + at : pair * 2 * TILE + at + WORDS, cut] = error.astype(jnp.bfloat16)
        scores = following
    write_rows(3)
    for section in range(sections):
        cut = slice(section * quarter, (section + 1) * quarter)
        col_ref[:, cut] = jnp.dot(cols_ref[...], error_ref[:, cut], preferred_element_type=jnp.float32)


def plane_total(came_ref):
    total = came_ref[0]
    for part in range(1, came_ref.shape[0]):
        total = total + came_ref[part]
    return total


def to_line_sum_kernel(came_ref, out_ref):
    total = plane_total(came_ref)
    deep = out_ref.shape[1]
    for part in range(out_ref.shape[0]):
        out_ref[part] = total[part * deep : (part + 1) * deep, :]


def to_owner_kernel(owners_ref, came_ref, out_ref):
    total = plane_total(came_ref)
    out_ref[...] = jnp.zeros_like(out_ref)
    quarter = out_ref.shape[2]
    for s in range(SECTIONS):
        out_ref[owners_ref[s]] = total[:, s * quarter : (s + 1) * quarter] * 0.125


def rows_kernel(scale, keep_ref, came_ref, out_ref, row_ref):
    quarter, width = out_ref.shape
    row = keep_ref[0] + came_ref[...]
    for tile in range(quarter // TILE):
        for plane in range(PLANES):
            at = tile * TILE + plane * WORDS
            for lane in range(width // 128):
                row_ref[lane, pl.ds(tile * TILE + plane, WORDS, stride=PLANES), :] = row[
                    at : at + WORDS, lane * 128 : (lane + 1) * 128
                ]
    for lane in range(width // 128):
        out_ref[:, lane * 128 : (lane + 1) * 128] = row_ref[lane, :quarter, :] * scale


def finish_kernel(scale, owners_ref, rows_ref, back_ref, out_ref):
    mine = lax.axis_index("blk")
    owned = jnp.bool_(False)
    for s in range(SECTIONS):
        owned = owned | (owners_ref[s] == mine)
    quarter, width = out_ref.shape

    @pl.when(owned)
    def _():
        out_ref[...] = rows_ref[...] + back_ref[...].reshape(width, quarter).T * (8.0 * scale)

    @pl.when(jnp.logical_not(owned))
    def _():
        out_ref[...] = rows_ref[...]


def body(embedding, adjacency, owners):
    rows, width = embedding.shape
    sections = adjacency.shape[0]
    groups = lax.axis_size("grp")
    blocks = lax.axis_size("blk")
    quarter = rows // groups
    wide = sections * quarter
    plane_xy = [[x * 32 + z * 4 + y for x in range(2) for y in range(4)] for z in range(LINE)]
    line_z = [[x * 32 + z * 4 + y for z in range(LINE)] for x in range(2) for y in range(4)]

    fence = lax.optimization_barrier

    def swap(value, line=None):
        return lax.all_to_all(value, "blk", 0, 0, axis_index_groups=line)

    def shape(*extent, dtype=jnp.float32):
        return jax.ShapeDtypeStruct(extent, dtype)

    half = jnp.bfloat16
    deep, lanes = 2 * quarter // blocks, width // 2
    own, owners = local_call(
        own_kernel,
        (shape(blocks, deep, lanes, dtype=half), shape(blocks, dtype=jnp.int32)),
        [ANYWHERE, ANYWHERE],
        [pltpu.VMEM((quarter, width), half), pltpu.SemaphoreType.DMA((2,))],
    )(owners, embedding)
    got = swap(own)
    sent = local_call(to_line_kernel, shape(LINE, sections, deep, lanes, dtype=half), [SCALARS, VECTORS])(owners, got)
    came = swap(sent, line_z)
    spread = local_call(to_plane_kernel, shape(LINE, LINE, sections, deep, lanes, dtype=half), [VECTORS])(came)
    pieces = swap(spread, plane_xy)

    keep, send, col = local_call(
        products_kernel,
        (shape(2, quarter, width), shape(2, quarter, width), shape(width, wide)),
        [VECTORS] * 3,
        [
            pltpu.VMEM((wide, width), half),
            pltpu.VMEM((rows, width), half),
            pltpu.VMEM((width, rows), half),
            pltpu.VMEM((rows, wide), half),
        ],
        pl.CostEstimate(flops=6 * rows * wide * width, bytes_accessed=9 << 20, transcendentals=rows * wide),
    )(embedding, pieces, adjacency)

    col = col.astype(jnp.float16).reshape(LINE, width // LINE, wide)
    col = fence(swap(fence(col), plane_xy))
    col, keep, send = fence((col.astype(jnp.float32), keep, send))
    col = local_call(to_line_sum_kernel, shape(LINE, width // blocks, wide), [VECTORS])(col)
    far = lax.ppermute(send.astype(jnp.float16), "grp", [(g, g ^ 2) for g in range(groups)])
    col = swap(col.astype(jnp.float16), line_z).astype(jnp.float32)
    col, far, keep = fence((col, far, keep))
    keep = keep + far.astype(jnp.float32)
    col = local_call(to_owner_kernel, shape(blocks, width // blocks, quarter), [SCALARS, VECTORS])(owners, col)
    far = lax.ppermute(keep[1].astype(jnp.float16), "grp", [(g, g ^ 1) for g in range(groups)]).astype(jnp.float32)
    back = swap(col.astype(jnp.float16)).astype(jnp.float32)
    scale = 0.5 * rows ** (-0.5)
    row = local_call(
        functools.partial(rows_kernel, scale),
        shape(quarter, width),
        [VECTORS] * 2,
        [pltpu.VMEM((width // 128, quarter + PLANES, 128), jnp.float32)],
    )(keep, far)
    return local_call(functools.partial(finish_kernel, scale), shape(quarter, width), [SCALARS, VECTORS, VECTORS])(
        owners, row, back
    )


def solution(mesh):
    return jax.shard_map(
        body,
        mesh=mesh,
        in_specs=(P("blk", None), P(None, "blk", "grp"), P()),
        out_specs=P(("blk", "grp"), None),
        check_vma=False,
    )
```
